32 devices in a mesh: row: 4 (over z), col: 8 (over y, x, core).
Axes of the slice: x: 2, y: 2, z: 4, core: 2. Of those that a mesh axis runs over, the one named last changes fastest.
Arguments:
- amplitudes: bfloat16 [192, 640000], P('col', 'row'), may hold values from -6 to 6
- integrals: bfloat16 [640000, 1600], P(('row', 'col')), may hold values from -0.0078125 to 0.0078125
- occ_irrep: int32 [120], replicated, may hold values from 0 to 7, as said below
- vir_irrep: int32 [800], replicated, may hold values from 0 to 7, as said below
- tile_owner: int32 [96], replicated, may hold values from 0 to 31, as said below
Outputs:
- inbox: bfloat16 [384, 1600], P(('row', 'col'))
The draws below stay inside these ranges and needn't reach their ends.
Inputs may be any that keep to these rules, and one draw needn't show every extreme that they name: `tile_owner`: no device owns more than 6 tiles and some device owns exactly 6; in every draw the 3 tiles of some device's rows of result all have one owner. `occ_irrep`: labels never decrease along the orbitals, so each irrep's orbitals form one contiguous block. Each of irreps 1 to 7 holds at least one and at most 2 orbitals, one of them exactly that most; irrep 0 holds all the others. `vir_irrep`: labels never decrease along the orbitals, so each irrep's orbitals form one contiguous block. Each of irreps 1 to 7 holds at least one and at most 13 orbitals, one of them exactly that most; irrep 0 holds all the others.
All inputs are finite; a program needn't handle non-finite values.
Results may differ from the reference program's by a relative error of at most 0.0014.
Values may be sent and summed in bfloat16 or wider, within the bound.
A program may use at most 192 MiB of HBM per device.

```python
import jax
import jax.numpy as jnp
from jax import lax

NO = 120
NV = 800
TR = 2
PAIRS = 192
CD = 640000
AB = 1600
TILES_DEV = 3
NT = 96
CAP = 6
N_ROW = 4
N_COL = 8
DEVICES = 32


def sorted_labels(key, count):
    minor_most = max(2, count // 60)
    keys = jax.random.split(key, 2)
    minor_sizes = jax.random.randint(keys[0], (7,), 1, minor_most + 1).astype(jnp.int32)
    fullest = jax.random.randint(keys[1], (), 0, 7).astype(jnp.int32)
    minor_sizes = jnp.where(jnp.arange(7, dtype=jnp.int32) == fullest, jnp.int32(minor_most), minor_sizes).astype(jnp.int32)
    running = jnp.cumsum(minor_sizes).astype(jnp.int32)
    minor_total = running[6]
    offsets = jnp.concatenate([jnp.zeros((1,), jnp.int32), running[:6]])
    starts = (count - minor_total + offsets).astype(jnp.int32)
    positions = jnp.arange(count, dtype=jnp.int32)
    return jnp.sum((positions[:, None] >= starts[None, :]).astype(jnp.int32), axis=1).astype(jnp.int32)


def draw_occ_irrep(key, part):
    return sorted_labels(jax.random.fold_in(key, 31), NO)


def draw_vir_irrep(key, part):
    return sorted_labels(jax.random.fold_in(key, 47), NV)


def draw_tile_owner(key, part):
    keys = jax.random.split(jax.random.fold_in(key, 17), 4)
    target = jax.random.randint(keys[0], (), 0, DEVICES).astype(jnp.int32)
    source = jax.random.randint(keys[1], (), 0, DEVICES).astype(jnp.int32)
    others = (jax.random.permutation(keys[2], DEVICES * CAP - CAP)[:NT - CAP] // CAP).astype(jnp.int32)
    others = others + (others >= target).astype(jnp.int32)
    labels = jnp.concatenate([jnp.full((CAP,), target, jnp.int32), others])
    remain = jax.random.permutation(keys[3], NT - TILES_DEV).astype(jnp.int32)
    remain = remain + TILES_DEV * (remain >= source * TILES_DEV).astype(jnp.int32)
    order = jnp.concatenate([source * TILES_DEV + jnp.arange(TILES_DEV, dtype=jnp.int32), remain])
    return jnp.zeros((NT,), jnp.int32).at[order].set(labels)


def raised(values, rng, source, target, blocks, factor):
    def block_of(axis_at):
        return (jnp.arange(values.shape[axis_at]) // (values.shape[axis_at] // blocks)).reshape((-1,) + (1,) * (values.ndim - 1 - axis_at))

    first = jax.random.permutation(rng, blocks)[block_of(target)]
    far = (block_of(target) + blocks // 2) % blocks
    return jnp.where((block_of(source) == first) | (block_of(source) == far), factor * values, values)


def steps_of(key, extent, cuts, low, largest):
    factor_of = 1.0
    for axis_at, shards_of in cuts:
        draws = jax.random.uniform(jax.random.fold_in(jax.random.fold_in(key, 6), axis_at), (shards_of,), jnp.float32, low / len(cuts), largest / len(cuts))
        factor_of = factor_of * jnp.repeat(jnp.exp(draws), extent[axis_at] // shards_of).reshape((-1,) + (1,) * (len(extent) - 1 - axis_at))
    return factor_of


def centred(rng, extent, scale, reach, cuts=(), kind=jnp.bfloat16):
    level = steps_of(rng, extent, cuts, -0.22, 0.18) if cuts else 1.0
    values = jax.random.normal(rng, extent, jnp.float32) * scale * level
    return jnp.minimum(jnp.maximum(values, -reach), reach).astype(kind)


def gaussian_with(key, extent, width, reach, cuts, heavy, kind=jnp.bfloat16):
    array = width * jax.random.normal(key, extent, jnp.float32)
    if cuts:
        array = array * steps_of(key, extent, cuts, -0.22, 0.18)
    return jnp.clip(raised(array, jax.random.fold_in(key, 3), *heavy), -reach, reach).astype(kind)


def setup_inputs(seed: int = 0) -> dict:
    streams_of = jax.random.split(jax.random.key(seed), 6)
    amplitudes = gaussian_with(streams_of[0], (PAIRS, CD), 1.0, 6.0, ((0, 8), (1, 4)), (1, 0, 8, 2.0))
    integrals = centred(streams_of[1], (CD, AB), CD ** -0.5, 0.0078125, ((0, 32),))
    occ_irrep = draw_occ_irrep(jax.random.fold_in(streams_of[5], 71), 0)
    vir_irrep = draw_vir_irrep(jax.random.fold_in(streams_of[5], 71), 0)
    tile_owner = draw_tile_owner(jax.random.fold_in(streams_of[5], 71), 0)
    return {"amplitudes": amplitudes, "integrals": integrals, "occ_irrep": occ_irrep, "vir_irrep": vir_irrep, "tile_owner": tile_owner}


def reference(amplitudes, integrals, occ_irrep, vir_irrep, tile_owner):
    pair_index = jnp.arange(PAIRS, dtype=jnp.int32)
    pair_irrep = jnp.bitwise_xor(occ_irrep[pair_index // NO], occ_irrep[pair_index % NO])
    ab_index = jnp.arange(AB, dtype=jnp.int32)
    ab_irrep = jnp.bitwise_xor(vir_irrep[ab_index // NV], vir_irrep[ab_index % NV])

    def accumulate(block, total):
        cd_irrep = jnp.bitwise_xor(vir_irrep[block], vir_irrep)
        start = (block * NV).astype(jnp.int32)
        panel = lax.dynamic_slice(amplitudes, (jnp.int32(0), start), (PAIRS, NV)).astype(jnp.float32)
        slab = lax.dynamic_slice(integrals, (start, jnp.int32(0)), (NV, AB)).astype(jnp.float32)
        masked_t = jnp.where(pair_irrep[:, None] == cd_irrep[None, :], panel, jnp.zeros((), jnp.float32))
        masked_v = jnp.where(cd_irrep[:, None] == ab_irrep[None, :], slab, jnp.zeros((), jnp.float32))
        return total + jnp.dot(masked_t, masked_v, precision=lax.Precision.HIGHEST)

    total = lax.fori_loop(0, NV, accumulate, jnp.zeros((PAIRS, AB), jnp.float32))
    result = total.astype(jnp.bfloat16)
    tiles = result.reshape(NT, TR * AB)
    tile_ids = jnp.arange(NT, dtype=jnp.int32)
    same = tile_owner[:, None] == tile_owner[None, :]
    earlier = tile_ids[:, None] > tile_ids[None, :]
    rank = jnp.sum(jnp.where(same & earlier, 1, 0), axis=1).astype(jnp.int32)
    slot = (tile_owner * CAP + rank).astype(jnp.int32)
    inbox = jnp.zeros((N_ROW * N_COL * CAP, TR * AB), jnp.bfloat16).at[slot].set(tiles)
    return inbox.reshape(N_ROW * N_COL * CAP * TR, AB)
```

```python
import functools

import jax
import jax.numpy as jnp
from jax import lax
from jax.experimental import pallas as pl
from jax.experimental.pallas import tpu as pltpu
from jax.sharding import PartitionSpec as P

TR = 2
CAP = 6
LABELS = 8
LANES = 128
AHEAD = 3
MESH = pl.DeviceIdType.MESH
F32 = jnp.float32
BF16 = jnp.bfloat16
I32 = jnp.int32


def cuts(tiles):
    width = max(1, min(20, tiles // 4))
    tail = [max(1, width // 2), max(1, width // 4)]
    rest = tiles - sum(tail)
    count = -(-rest // width)
    sizes = [rest // count + (1 if k < rest % count else 0) for k in range(count)] + tail
    borders = [0]
    for size in sizes:
        borders.append(borders[-1] + size)
    return borders


def label_of(index, firsts):
    total = jnp.zeros(index.shape, I32)
    for first in firsts:
        total = total + jnp.where(index >= first, 1, 0)
    return total


def firsts_of(labels):
    return [
        jnp.sum(jnp.where(labels < g, 1.0, 0.0), axis=1, keepdims=True).astype(I32)
        for g in range(1, LABELS)
    ]


def split_index(start, offset, size, most):
    high = lax.div(start, jnp.int32(size))
    low = start - high * size + offset
    step = jnp.zeros(offset.shape, I32)
    for k in range(1, (size + most) // size + 1):
        step = step + jnp.where(low >= k * size, 1, 0)
    return high + step, low - step * size


def kernel(
    nrow, ncol, width, amp, vt, vedge, occ, vir, owner, out,
    held, masked, slab, acc, part, near, plane, psum, line, lined, whole, ready, plab,
    sent, got, mine, vsem, s1, r1, s2, r2, s3, r3, s4, r4, s5, r5, s6, r6,
):
    local = amp.shape[0]
    abw, cdw = vt.shape
    pairs = local * ncol
    nvirt = vir.shape[1]
    norb = occ.shape[1]
    chips = ncol // 2
    abt = psum.shape[1] // LANES
    zt = line.shape[2] // LANES
    np_ = masked.shape[0]
    mrow = lax.axis_index("row")
    mcol = lax.axis_index("col")
    core = lax.rem(mcol, 2)
    chip = lax.div(mcol, 2)
    me = mrow * ncol + mcol
    borders = cuts(width // LANES)
    count = len(borders) - 1

    def col_of(k):
        return lax.rem(mcol + k, ncol)

    def row_of(k):
        return lax.rem(mrow + k, nrow)

    def chip_of(k):
        return lax.rem(chip + k, chips)

    barrier = pltpu.get_barrier_semaphore()
    for k in range(1, ncol):
        pl.semaphore_signal(barrier, inc=1, device_id=(mrow, col_of(k)), device_id_type=MESH)
    for k in range(1, nrow):
        pl.semaphore_signal(barrier, inc=1, device_id=(row_of(k), mcol), device_id_type=MESH)
    pl.semaphore_wait(barrier, ncol - 1 + nrow - 1)

    def shift_of(col):
        return lax.rem(col * cdw, LANES)

    def span(q):
        low = 0 if q == 0 else (borders[q] + 1) * LANES
        high = min((borders[q + 1] + 1) * LANES, width)
        return low, high - low

    def amp_slice(col, q):
        low, size = span(q)
        start = pl.multiple_of(col * cdw - shift_of(col) + low, LANES)
        return amp.at[:, pl.ds(start, size)]

    def sends(q):
        low, size = span(q)
        return [
            pltpu.make_async_remote_copy(
                src_ref=amp_slice(col_of(k), q),
                dst_ref=held.at[mcol, :, pl.ds(low, size)],
                send_sem=sent.at[q, k - 1],
                recv_sem=got.at[q, k - 1],
                device_id=(mrow, col_of(k)),
                device_id_type=MESH,
            )
            for k in range(1, ncol)
        ]

    def own(q):
        low, size = span(q)
        return pltpu.make_async_copy(
            amp_slice(mcol, q), held.at[mcol, :, pl.ds(low, size)], mine.at[q]
        )

    class Slab:
        def __init__(self, q):
            low = borders[q] * LANES
            size = min(borders[q + 1] * LANES, cdw // LANES * LANES) - low
            self.copies = []
            if size:
                self.copies.append(pltpu.make_async_copy(
                    vt.at[:, pl.ds(low, size)], slab.at[q % 2, :, pl.ds(0, size)], vsem.at[q % 2]
                ))
            if low + size < borders[q + 1] * LANES:
                self.copies.append(pltpu.make_async_copy(
                    vedge, slab.at[q % 2, :, pl.ds(size, LANES)], vsem.at[2]
                ))

        def start(self):
            for copy in self.copies:
                copy.start()

        def wait(self):
            for copy in self.copies:
                copy.wait()

    slab_copy = Slab

    def launch(q):
        for copy in sends(q):
            copy.start()
        own(q).start()

    for q in range(min(AHEAD, count)):
        launch(q)
    slab_copy(0).start()
    if count > 1:
        slab_copy(1).start()

    occ_firsts = firsts_of(occ[...])
    vir_firsts = firsts_of(vir[...])
    row_id = lax.broadcasted_iota(I32, (pairs, LANES), 0)
    first, second = split_index(jnp.int32(0), row_id, norb, pairs)
    plab[...] = jnp.bitwise_xor(label_of(first, occ_firsts), label_of(second, occ_firsts))

    acc[...] = jnp.zeros_like(acc)
    masked[...] = jnp.zeros_like(masked)

    tiles = owner.shape[1]
    is_mine = jnp.where(jnp.broadcast_to(owner[...], (16, tiles)) == me, 1.0, 0.0).astype(BF16)
    tile_id = lax.broadcasted_iota(I32, (tiles, pairs), 0)
    pair_tile = lax.broadcasted_iota(I32, (tiles, pairs), 1) // TR
    spread = jnp.where(tile_id == pair_tile, 1.0, 0.0).astype(BF16)
    before = jnp.where(tile_id < pair_tile, 1.0, 0.0).astype(BF16)
    mine_of = jnp.dot(is_mine, spread, preferred_element_type=F32)
    rank_of = jnp.dot(is_mine, before, preferred_element_type=F32)
    pair_id = lax.broadcasted_iota(I32, (16, pairs), 1)
    place = rank_of.astype(I32) * TR + (pair_id - (pair_id // TR) * TR)
    picker = jnp.where(
        (mine_of > 0.5) & (place == lax.broadcasted_iota(I32, (16, pairs), 0)), 1.0, 0.0
    ).astype(BF16)

    shift = shift_of(mcol)
    turn = lax.rem(LANES - shift, LANES)
    lane = lax.broadcasted_iota(I32, (local, LANES), 1)
    from_here = lane < LANES - shift

    for q in range(count):
        size = borders[q + 1] - borders[q]
        for copy in sends(q):
            copy.wait()
        own(q).wait()
        if q + AHEAD < count:
            launch(q + AHEAD)
        base = me * cdw + borders[q] * LANES
        offset = lax.broadcasted_iota(I32, (1, size * LANES), 1)
        high, low = split_index(base, offset, nvirt, size * LANES)
        cd_label = jnp.bitwise_xor(label_of(high, vir_firsts), label_of(low, vir_firsts))
        inside = offset + borders[q] * LANES < cdw
        cd_label = jnp.where(inside, cd_label, -1)

        def prepare(s, carry, size=size, q=q, cd_label=cd_label):
            halves = []
            for h in range(2):
                src = s * 2 + h
                label = plab[pl.ds(pl.multiple_of(src * local, 8), local), :]
                turned = []
                for j in range(size + 1):
                    tile = borders[q] + j
                    if (tile + 1) * LANES > width:
                        turned.append(turned[-1])
                        continue
                    value = held[src, :, tile * LANES:(tile + 1) * LANES].astype(F32)
                    turned.append(pltpu.roll(value, turn, 1))
                columns = []
                for j in range(size):
                    value = jnp.where(from_here, turned[j], turned[j + 1])
                    keep = cd_label[:, j * LANES:(j + 1) * LANES] == label
                    columns.append(jnp.where(keep, value, 0.0))
                halves.append(columns)
            for j in range(size):
                both = jnp.concatenate([halves[0][j], halves[1][j]], axis=0).astype(BF16)
                start = pl.multiple_of(s * (2 * local), 16)
                masked[pl.ds(start, 2 * local), j * LANES:(j + 1) * LANES] = both
            return carry

        lax.fori_loop(0, chips, prepare, 0)
        slab_copy(q).wait()
        step = 320 if abw % 320 == 0 else abw

        def multiply(m, carry, size=size, q=q, step=step):
            rows = pl.ds(pl.multiple_of(m * step, 16), step)
            acc[rows, :] += lax.dot_general(
                slab[q % 2, rows, 0:size * LANES],
                masked[:, 0:size * LANES],
                (((1,), (1,)), ((), ())),
                preferred_element_type=F32,
            )
            return carry

        lax.fori_loop(0, abw // step, multiply, 0)
        if q + 2 < count:
            slab_copy(q + 2).start()

    for j in range(abt):
        block = acc[j * LANES:(j + 1) * LANES, :].T
        for c in range(ncol):
            part[c % 2, c // 2, :, j * LANES:(j + 1) * LANES] = block[c * local:(c + 1) * local, :]

    other = mrow, chip * 2 + 1 - core
    first_sends = []
    for k in list(range(1, chips)) + [0]:
        copy = pltpu.make_async_remote_copy(
            src_ref=part.at[1 - core, chip_of(k)], dst_ref=near.at[chip_of(k)],
            send_sem=s1.at[k], recv_sem=r1.at[k], device_id=other, device_id_type=MESH,
        )
        copy.start()
        first_sends.append(copy)
    plane_sends = []
    for copy, k in zip(first_sends, list(range(1, chips)) + [0]):
        copy.wait_recv()
        part[core, chip_of(k)] += near[chip_of(k)]
        if k:
            over = pltpu.make_async_remote_copy(
                src_ref=part.at[core, chip_of(k)], dst_ref=plane.at[k - 1],
                send_sem=s2.at[k - 1], recv_sem=r2.at[k - 1],
                device_id=(mrow, chip_of(k) * 2 + core), device_id_type=MESH,
            )
            over.start()
            plane_sends.append(over)
    total = part[core, chip]
    for k, copy in enumerate(plane_sends):
        copy.wait_recv()
        total = total + plane[k]
    psum[...] = total

    def lanes_of(row):
        return pl.multiple_of(jnp.minimum(row * zt, abt - zt) * LANES, LANES)

    row_sends = []
    for k in range(1, nrow):
        copy = pltpu.make_async_remote_copy(
            src_ref=psum.at[:, pl.ds(lanes_of(row_of(k)), zt * LANES)], dst_ref=line.at[k - 1],
            send_sem=s3.at[k - 1], recv_sem=r3.at[k - 1],
            device_id=(row_of(k), mcol), device_id_type=MESH,
        )
        copy.start()
        row_sends.append(copy)
    ab = lanes_of(mrow) + lax.broadcasted_iota(I32, (1, zt * LANES), 1)
    ab_first, ab_second = split_index(jnp.int32(0), ab, nvirt, abt * LANES)
    ab_label = jnp.bitwise_xor(
        label_of(ab_first, vir_firsts), label_of(ab_second, vir_firsts)
    )
    my_label = plab[pl.ds(pl.multiple_of(mcol * local, 8), local), :]
    my_label = jnp.concatenate([my_label] * zt, axis=1)
    summed = psum[:, pl.ds(lanes_of(mrow), zt * LANES)]
    for k, copy in enumerate(row_sends):
        copy.wait_recv()
        summed = summed + line[k]
    lined[mrow] = jnp.where(ab_label == my_label, summed, 0.0).astype(BF16)

    back = []
    for k in range(1, nrow):
        copy = pltpu.make_async_remote_copy(
            src_ref=lined.at[mrow], dst_ref=lined.at[mrow],
            send_sem=s4.at[k - 1], recv_sem=r4.at[k - 1],
            device_id=(row_of(k), mcol), device_id_type=MESH,
        )
        copy.start()
        back.append(copy)
    for copy in back:
        copy.wait_recv()
    for r in range(nrow):
        low = min(r * zt, abt - zt) * LANES
        whole[core, chip, :, low:low + zt * LANES] = lined[r]
    over = []
    for k in range(1, chips):
        copy = pltpu.make_async_remote_copy(
            src_ref=whole.at[core, chip], dst_ref=whole.at[core, chip],
            send_sem=s5.at[k - 1], recv_sem=r5.at[k - 1],
            device_id=(mrow, chip_of(k) * 2 + core), device_id_type=MESH,
        )
        copy.start()
        over.append(copy)
    across = []
    for k in range(chips):
        src = lax.rem(chip - k + chips, chips)
        if k:
            over[k - 1].wait_recv()
        copy = pltpu.make_async_remote_copy(
            src_ref=whole.at[core, src], dst_ref=whole.at[core, src],
            send_sem=s6.at[k], recv_sem=r6.at[k], device_id=other, device_id_type=MESH,
        )
        copy.start()
        across.append(copy)
    for copy in across:
        copy.wait_recv()
    for c in range(chips):
        both = jnp.concatenate([whole[0, c].astype(F32), whole[1, c].astype(F32)], axis=0)
        ready[c * 2 * local:(c + 1) * 2 * local, :] = both.astype(BF16)
    picked = jnp.dot(picker, ready[...], preferred_element_type=F32)
    out[...] = picked[0:CAP * TR, 0:abw].astype(BF16)
    for copy in first_sends + plane_sends + row_sends + back + over + across:
        copy.wait_send()


def on_device(amplitudes, integrals, occ_irrep, vir_irrep, tile_owner):
    ncol = lax.axis_size("col")
    nrow = lax.axis_size("row")
    local, cd_row = amplitudes.shape
    cdw, abw = integrals.shape
    pairs = local * ncol
    chips = ncol // 2
    most = max((c * cdw) % LANES for c in range(ncol))
    width = -(-(cdw + most) // LANES) * LANES
    for c in range(ncol):
        assert c * cdw - (c * cdw) % LANES + width <= cd_row
    borders = cuts(width // LANES)
    count = len(borders) - 1
    widest = max(b - a for a, b in zip(borders, borders[1:])) * LANES
    abt = -(-abw // LANES)
    zt = -(-abt // nrow)
    padded = -(-pairs // LANES) * LANES
    assert width - LANES < cdw < width
    edge = jnp.pad(integrals[width - LANES:, :].T, ((0, 0), (0, width - cdw)))
    vmem = pl.BlockSpec(memory_space=pltpu.VMEM)
    hbm = pl.BlockSpec(memory_space=pl.ANY)

    def dma(*shape):
        return pltpu.SemaphoreType.DMA(shape)

    stages = [chips, chips - 1, nrow - 1, nrow - 1, chips - 1, chips]
    return pl.pallas_call(
        functools.partial(kernel, nrow, ncol, width),
        out_shape=jax.ShapeDtypeStruct((CAP * TR, abw), BF16),
        in_specs=[hbm, hbm, hbm, vmem, vmem, vmem],
        out_specs=vmem,
        scratch_shapes=[
            pltpu.VMEM((ncol, local, width), BF16),
            pltpu.VMEM((padded, widest), BF16),
            pltpu.VMEM((2, abw, widest), BF16),
            pltpu.VMEM((abt * LANES, padded), F32),
            pltpu.VMEM((2, chips, local, abt * LANES), F32),
            pltpu.VMEM((chips, local, abt * LANES), F32),
            pltpu.VMEM((chips - 1, local, abt * LANES), F32),
            pltpu.VMEM((local, abt * LANES), F32),
            pltpu.VMEM((nrow - 1, local, zt * LANES), F32),
            pltpu.VMEM((nrow, local, zt * LANES), BF16),
            pltpu.VMEM((2, chips, local, abt * LANES), BF16),
            pltpu.VMEM((pairs, abt * LANES), BF16),
            pltpu.VMEM((pairs, LANES), I32),
            dma(count, ncol - 1),
            dma(count, ncol - 1),
            dma(count),
            dma(3),
        ]
        + [dma(n) for n in stages for _ in range(2)],
        compiler_params=pltpu.CompilerParams(
            collective_id=0, has_side_effects=True, vmem_limit_bytes=60 * 1024 * 1024
        ),
        cost_estimate=pl.CostEstimate(
            flops=2 * pairs * cdw * abw, bytes_accessed=2 * cdw * abw, transcendentals=0
        ),
    )(
        amplitudes,
        integrals.T,
        edge,
        occ_irrep.reshape(1, -1),
        vir_irrep.reshape(1, -1),
        tile_owner.reshape(1, -1),
    )


def solution(mesh):
    in_specs = (P("col", "row"), P(("row", "col"), None), P(), P(), P())
    out_specs = P(("row", "col"), None)
    return jax.shard_map(
        on_device, mesh=mesh, in_specs=in_specs, out_specs=out_specs, check_vma=False
    )
```

```python
import functools

import jax
import jax.numpy as jnp
from jax import lax
from jax.experimental import pallas as pl
from jax.experimental.pallas import tpu as pltpu
from jax.sharding import PartitionSpec as P

TR = 2
CAP = 6
LABELS = 8
LANES = 128
AHEAD = 3
MESH = pl.DeviceIdType.MESH
F32 = jnp.float32
BF16 = jnp.bfloat16
I32 = jnp.int32


def cuts(tiles):
    width = max(1, min(20, tiles // 4))
    tail = [max(1, width // 2), max(1, width // 4)]
    rest = tiles - sum(tail)
    count = -(-rest // width)
    sizes = [rest // count + (1 if k < rest % count else 0) for k in range(count)] + tail
    borders = [0]
    for size in sizes:
        borders.append(borders[-1] + size)
    return borders


def label_of(index, firsts):
    total = jnp.zeros(index.shape, I32)
    for first in firsts:
        total = total + jnp.where(index >= first, 1, 0)
    return total


def firsts_of(labels):
    return [
        jnp.sum(jnp.where(labels < g, 1.0, 0.0), axis=1, keepdims=True).astype(I32)
        for g in range(1, LABELS)
    ]


def count_below(labels, g):
    total = labels.shape[0]
    low = jnp.int32(0)
    bit = 1 << (total.bit_length() - 1)
    while bit:
        tried = low + bit
        under = labels[jnp.minimum(tried, total) - 1] < g
        low = jnp.where(under & (tried <= total), tried, low)
        bit //= 2
    return low


def split_index(start, offset, size, most):
    high = lax.div(start, jnp.int32(size))
    low = start - high * size + offset
    step = jnp.zeros(offset.shape, I32)
    for k in range(1, (size + most) // size + 1):
        step = step + jnp.where(low >= k * size, 1, 0)
    return high + step, low - step * size


def kernel(
    nrow, ncol, width, amp, vt, vedge, occ, vir, owner, out,
    held, masked, slab, acc, part, near, plane, psum, line, lined, whole, ready, plab,
    sent, got, mine, vsem, s1, r1, s2, r2, s3, r3, s4, r4, s5, r5, s6, r6,
):
    local = amp.shape[0]
    abw, cdw = vt.shape
    pairs = local * ncol
    nvirt = vir.shape[0]
    norb = occ.shape[1]
    chips = ncol // 2
    abt = psum.shape[1] // LANES
    zt = line.shape[2] // LANES
    np_ = masked.shape[0]
    mrow = lax.axis_index("row")
    mcol = lax.axis_index("col")
    core = lax.rem(mcol, 2)
    chip = lax.div(mcol, 2)
    me = mrow * ncol + mcol
    borders = cuts(width // LANES)
    count = len(borders) - 1

    def col_of(k):
        col = mcol
        bit = 1
        while bit < ncol:
            if (k // bit) % 2:
                col = col + bit - 2 * bit * lax.rem(lax.div(mcol, bit), 2)
            bit *= 2
        return col

    order = list(range(2, ncol, 2)) + list(range(3, ncol, 2)) + [1]

    def row_of(k):
        return lax.rem(mrow + k, nrow)

    def chip_of(k):
        return lax.rem(chip + k, chips)

    barrier = pltpu.get_barrier_semaphore()
    for k in range(1, ncol):
        pl.semaphore_signal(barrier, inc=1, device_id=(mrow, col_of(k)), device_id_type=MESH)
    for k in range(1, nrow):
        pl.semaphore_signal(barrier, inc=1, device_id=(row_of(k), mcol), device_id_type=MESH)
    pl.semaphore_wait(barrier, ncol - 1 + nrow - 1)

    def shift_of(col):
        return lax.rem(col * cdw, LANES)

    def span(q):
        low = 0 if q == 0 else (borders[q] + 1) * LANES
        high = min((borders[q + 1] + 1) * LANES, width)
        return low, high - low

    def amp_slice(col, q):
        low, size = span(q)
        start = pl.multiple_of(col * cdw - shift_of(col) + low, LANES)
        return amp.at[:, pl.ds(start, size)]

    def sends(q):
        low, size = span(q)
        return [
            pltpu.make_async_remote_copy(
                src_ref=amp_slice(col_of(k), q),
                dst_ref=held.at[mcol, :, pl.ds(low, size)],
                send_sem=sent.at[q, k - 1],
                recv_sem=got.at[q, k - 1],
                device_id=(mrow, col_of(k)),
                device_id_type=MESH,
            )
            for k in order
        ]

    def own(q):
        low, size = span(q)
        return pltpu.make_async_copy(
            amp_slice(mcol, q), held.at[mcol, :, pl.ds(low, size)], mine.at[q]
        )

    class Slab:
        def __init__(self, q):
            low = borders[q] * LANES
            size = min(borders[q + 1] * LANES, cdw // LANES * LANES) - low
            self.copies = []
            if size:
                self.copies.append(pltpu.make_async_copy(
                    vt.at[:, pl.ds(low, size)], slab.at[q % 2, :, pl.ds(0, size)], vsem.at[q % 2]
                ))

        def start(self):
            for copy in self.copies:
                copy.start()

        def wait(self):
            for copy in self.copies:
                copy.wait()

    slab_copy = Slab

    def launch(q):
        for copy in sends(q):
            copy.start()
        own(q).start()

    for q in range(min(AHEAD, count)):
        launch(q)
    slab_copy(0).start()
    if count > 1:
        slab_copy(1).start()

    occ_firsts = firsts_of(occ[...])
    vir_firsts = [count_below(vir, g) for g in range(1, LABELS)]
    row_id = lax.broadcasted_iota(I32, (pairs, LANES), 0)
    first, second = split_index(jnp.int32(0), row_id, norb, pairs)
    plab[...] = jnp.bitwise_xor(label_of(first, occ_firsts), label_of(second, occ_firsts))

    acc[...] = jnp.zeros_like(acc)
    masked[...] = jnp.zeros_like(masked)

    tiles = owner.shape[1]
    is_mine = jnp.where(jnp.broadcast_to(owner[...], (16, tiles)) == me, 1.0, 0.0).astype(BF16)
    tile_id = lax.broadcasted_iota(I32, (tiles, pairs), 0)
    pair_tile = lax.broadcasted_iota(I32, (tiles, pairs), 1) // TR
    spread = jnp.where(tile_id == pair_tile, 1.0, 0.0).astype(BF16)
    before = jnp.where(tile_id < pair_tile, 1.0, 0.0).astype(BF16)
    mine_of = jnp.dot(is_mine, spread, preferred_element_type=F32)
    rank_of = jnp.dot(is_mine, before, preferred_element_type=F32)
    pair_id = lax.broadcasted_iota(I32, (16, pairs), 1)
    place = rank_of.astype(I32) * TR + (pair_id - (pair_id // TR) * TR)
    picker = jnp.where(
        (mine_of > 0.5) & (place == lax.broadcasted_iota(I32, (16, pairs), 0)), 1.0, 0.0
    ).astype(BF16)

    shift = shift_of(mcol)
    turn = lax.rem(LANES - shift, LANES)
    lane = lax.broadcasted_iota(I32, (local, LANES), 1)
    from_here = lane < LANES - shift

    for q in range(count):
        size = borders[q + 1] - borders[q]
        for copy in sends(q):
            copy.wait()
        own(q).wait()
        if q + AHEAD < count:
            launch(q + AHEAD)
        base = me * cdw + borders[q] * LANES
        offset = lax.broadcasted_iota(I32, (1, size * LANES), 1)
        high, low = split_index(base, offset, nvirt, size * LANES)
        cd_label = jnp.bitwise_xor(label_of(high, vir_firsts), label_of(low, vir_firsts))
        inside = offset + borders[q] * LANES < cdw
        cd_label = jnp.where(inside, cd_label, -1)

        def prepare(s, carry, size=size, q=q, cd_label=cd_label):
            halves = []
            for h in range(2):
                src = s * 2 + h
                label = plab[pl.ds(pl.multiple_of(src * local, 8), local), :]
                turned = []
                for j in range(size + 1):
                    tile = borders[q] + j
                    if (tile + 1) * LANES > width:
                        turned.append(turned[-1])
                        continue
                    value = held[src, :, tile * LANES:(tile + 1) * LANES].astype(F32)
                    turned.append(pltpu.roll(value, turn, 1))
                columns = []
                for j in range(size):
                    value = jnp.where(from_here, turned[j], turned[j + 1])
                    keep = cd_label[:, j * LANES:(j + 1) * LANES] == label
                    columns.append(jnp.where(keep, value, 0.0))
                halves.append(columns)
            for j in range(size):
                both = jnp.concatenate([halves[0][j], halves[1][j]], axis=0).astype(BF16)
                start = pl.multiple_of(s * (2 * local), 16)
                masked[pl.ds(start, 2 * local), j * LANES:(j + 1) * LANES] = both
            return carry

        lax.fori_loop(0, chips, prepare, 0)
        slab_copy(q).wait()
        if borders[q + 1] * LANES > cdw:
            edge = (size - 1) * LANES
            slab[q % 2, :, edge:edge + LANES] = jnp.zeros((abw, LANES), BF16)
            slab[q % 2, :, edge:edge + vedge.shape[1]] = vedge[...]
        step = 320 if abw % 320 == 0 else abw

        def multiply(m, carry, size=size, q=q, step=step):
            rows = pl.ds(pl.multiple_of(m * step, 16), step)
            acc[rows, :] += lax.dot_general(
                slab[q % 2, rows, 0:size * LANES],
                masked[:, 0:size * LANES],
                (((1,), (1,)), ((), ())),
                preferred_element_type=F32,
            )
            return carry

        lax.fori_loop(0, abw // step, multiply, 0)
        if q + 2 < count:
            slab_copy(q + 2).start()

    for j in range(abt):
        block = acc[j * LANES:(j + 1) * LANES, :].T
        for c in range(ncol):
            part[c % 2, c // 2, :, j * LANES:(j + 1) * LANES] = block[c * local:(c + 1) * local, :]

    other = mrow, chip * 2 + 1 - core
    first_sends = []
    for k in list(range(1, chips)) + [0]:
        copy = pltpu.make_async_remote_copy(
            src_ref=part.at[1 - core, chip_of(k)], dst_ref=near.at[chip_of(k)],
            send_sem=s1.at[k], recv_sem=r1.at[k], device_id=other, device_id_type=MESH,
        )
        copy.start()
        first_sends.append(copy)
    plane_sends = []
    for copy, k in zip(first_sends, list(range(1, chips)) + [0]):
        copy.wait_recv()
        part[core, chip_of(k)] += near[chip_of(k)]
        if k:
            over = pltpu.make_async_remote_copy(
                src_ref=part.at[core, chip_of(k)], dst_ref=plane.at[k - 1],
                send_sem=s2.at[k - 1], recv_sem=r2.at[k - 1],
                device_id=(mrow, chip_of(k) * 2 + core), device_id_type=MESH,
            )
            over.start()
            plane_sends.append(over)
    total = part[core, chip]
    for k, copy in enumerate(plane_sends):
        copy.wait_recv()
        total = total + plane[k]
    psum[...] = total

    def lanes_of(row):
        return pl.multiple_of(jnp.minimum(row * zt, abt - zt) * LANES, LANES)

    row_sends = []
    for k in range(1, nrow):
        copy = pltpu.make_async_remote_copy(
            src_ref=psum.at[:, pl.ds(lanes_of(row_of(k)), zt * LANES)], dst_ref=line.at[k - 1],
            send_sem=s3.at[k - 1], recv_sem=r3.at[k - 1],
            device_id=(row_of(k), mcol), device_id_type=MESH,
        )
        copy.start()
        row_sends.append(copy)
    ab = lanes_of(mrow) + lax.broadcasted_iota(I32, (1, zt * LANES), 1)
    ab_first, ab_second = split_index(jnp.int32(0), ab, nvirt, abt * LANES)
    ab_label = jnp.bitwise_xor(
        label_of(ab_first, vir_firsts), label_of(ab_second, vir_firsts)
    )
    my_label = plab[pl.ds(pl.multiple_of(mcol * local, 8), local), :]
    my_label = jnp.concatenate([my_label] * zt, axis=1)
    summed = psum[:, pl.ds(lanes_of(mrow), zt * LANES)]
    for k, copy in enumerate(row_sends):
        copy.wait_recv()
        summed = summed + line[k]
    lined[mrow] = jnp.where(ab_label == my_label, summed, 0.0).astype(BF16)

    back = []
    for k in range(1, nrow):
        copy = pltpu.make_async_remote_copy(
            src_ref=lined.at[mrow], dst_ref=lined.at[mrow],
            send_sem=s4.at[k - 1], recv_sem=r4.at[k - 1],
            device_id=(row_of(k), mcol), device_id_type=MESH,
        )
        copy.start()
        back.append(copy)
    for copy in back:
        copy.wait_recv()
    for r in range(nrow):
        low = min(r * zt, abt - zt) * LANES
        whole[core, chip, :, low:low + zt * LANES] = lined[r]
    over = []
    for k in range(1, chips):
        copy = pltpu.make_async_remote_copy(
            src_ref=whole.at[core, chip], dst_ref=whole.at[core, chip],
            send_sem=s5.at[k - 1], recv_sem=r5.at[k - 1],
            device_id=(mrow, chip_of(k) * 2 + core), device_id_type=MESH,
        )
        copy.start()
        over.append(copy)
    across = []
    for k in range(chips):
        src = lax.rem(chip - k + chips, chips)
        if k:
            over[k - 1].wait_recv()
        copy = pltpu.make_async_remote_copy(
            src_ref=whole.at[core, src], dst_ref=whole.at[core, src],
            send_sem=s6.at[k], recv_sem=r6.at[k], device_id=other, device_id_type=MESH,
        )
        copy.start()
        across.append(copy)
    for copy in across:
        copy.wait_recv()
    for c in range(chips):
        both = jnp.concatenate([whole[0, c].astype(F32), whole[1, c].astype(F32)], axis=0)
        ready[c * 2 * local:(c + 1) * 2 * local, :] = both.astype(BF16)
    picked = jnp.dot(picker, ready[...], preferred_element_type=F32)
    out[...] = picked[0:CAP * TR, 0:abw].astype(BF16)
    for copy in first_sends + plane_sends + row_sends + back + over + across:
        copy.wait_send()


def on_device(amplitudes, integrals, occ_irrep, vir_irrep, tile_owner):
    ncol = lax.axis_size("col")
    nrow = lax.axis_size("row")
    local, cd_row = amplitudes.shape
    cdw, abw = integrals.shape
    assert ncol & (ncol - 1) == 0
    pairs = local * ncol
    chips = ncol // 2
    most = max((c * cdw) % LANES for c in range(ncol))
    width = -(-(cdw + most) // LANES) * LANES
    for c in range(ncol):
        assert c * cdw - (c * cdw) % LANES + width <= cd_row
    borders = cuts(width // LANES)
    count = len(borders) - 1
    widest = max(b - a for a, b in zip(borders, borders[1:])) * LANES
    abt = -(-abw // LANES)
    zt = -(-abt // nrow)
    padded = -(-pairs // LANES) * LANES
    assert width - LANES < cdw < width
    edge = integrals[width - LANES:, :].T
    vmem = pl.BlockSpec(memory_space=pltpu.VMEM)
    hbm = pl.BlockSpec(memory_space=pl.ANY)
    smem = pl.BlockSpec(memory_space=pltpu.SMEM)

    def dma(*shape):
        return pltpu.SemaphoreType.DMA(shape)

    stages = [chips, chips - 1, nrow - 1, nrow - 1, chips - 1, chips]
    return pl.pallas_call(
        functools.partial(kernel, nrow, ncol, width),
        out_shape=jax.ShapeDtypeStruct((CAP * TR, abw), BF16),
        in_specs=[hbm, hbm, vmem, vmem, smem, vmem],
        out_specs=vmem,
        scratch_shapes=[
            pltpu.VMEM((ncol, local, width), BF16),
            pltpu.VMEM((padded, widest), BF16),
            pltpu.VMEM((2, abw, widest), BF16),
            pltpu.VMEM((abt * LANES, padded), F32),
            pltpu.VMEM((2, chips, local, abt * LANES), F32),
            pltpu.VMEM((chips, local, abt * LANES), F32),
            pltpu.VMEM((chips - 1, local, abt * LANES), F32),
            pltpu.VMEM((local, abt * LANES), F32),
            pltpu.VMEM((nrow - 1, local, zt * LANES), F32),
            pltpu.VMEM((nrow, local, zt * LANES), BF16),
            pltpu.VMEM((2, chips, local, abt * LANES), BF16),
            pltpu.VMEM((pairs, abt * LANES), BF16),
            pltpu.VMEM((pairs, LANES), I32),
            dma(count, ncol - 1),
            dma(count, ncol - 1),
            dma(count),
            dma(2),
        ]
        + [dma(n) for n in stages for _ in range(2)],
        compiler_params=pltpu.CompilerParams(
            collective_id=0, has_side_effects=True, vmem_limit_bytes=60 * 1024 * 1024
        ),
        cost_estimate=pl.CostEstimate(
            flops=2 * pairs * cdw * abw, bytes_accessed=2 * cdw * abw, transcendentals=0
        ),
    )(
        amplitudes,
        integrals.T,
        edge,
        occ_irrep.reshape(1, -1),
        vir_irrep,
        tile_owner.reshape(1, -1),
    )


def solution(mesh):
    in_specs = (P("col", "row"), P(("row", "col"), None), P(), P(), P())
    out_specs = P(("row", "col"), None)
    return jax.shard_map(
        on_device, mesh=mesh, in_specs=in_specs, out_specs=out_specs, check_vma=False
    )
```
